512 devices in a mesh: dp: 16 (over x, y_lo, core), mp: 32 (over z, y_hi).
Axes of the slice: x: 4, y: 4 (y_hi: 2, y_lo: 2; y = y_hi * 2 + y_lo), z: 16, core: 2. Of those that a mesh axis runs over, the one named last changes fastest.
Arguments:
- up_partials: bfloat16 [16, 32, 512, 512], P('dp', None, 'mp'), may hold values from -1.5 to 1.5
- down_partials: bfloat16 [16, 32, 512, 512], P('dp', None, 'mp'), may hold values from -1.5 to 1.5
- up_left: bfloat16 [32, 512, 512], P('mp'), may hold values from -0.25 to 0.25
- up_right: bfloat16 [32, 512, 512], P('mp'), may hold values from -0.25 to 0.25
- down_left: bfloat16 [32, 512, 512], P('mp'), may hold values from -0.25 to 0.25
- down_right: bfloat16 [32, 512, 512], P('mp'), may hold values from -0.25 to 0.25
- up_first: float32 [32, 512, 512], P('mp', 'dp'), may hold values from -4 to 4
- up_second: float32 [32, 512, 512], P('mp', 'dp'), may hold values from 0.2 to 2
- down_first: float32 [32, 512, 512], P('mp', 'dp'), may hold values from -4 to 4
- down_second: float32 [32, 512, 512], P('mp', 'dp'), may hold values from 0.2 to 2
Outputs:
- up_first_new: float32 [32, 512, 512], P('mp', 'dp')
- up_second_new: float32 [32, 512, 512], P('mp', 'dp')
- down_first_new: float32 [32, 512, 512], P('mp', 'dp')
- down_second_new: float32 [32, 512, 512], P('mp', 'dp')
- up_update: bfloat16 [32, 512, 512], P(None, 'mp', 'dp')
- down_update: bfloat16 [32, 512, 512], P(None, 'mp', 'dp')
The draws below stay inside these ranges and needn't reach their ends.
All inputs are finite; a program needn't handle non-finite values.
Results may differ from the reference program's by a relative error of at most 0.013.
Values may be sent and summed in bfloat16 or wider, within the bound.
No kernel may reach another device: no remote copies, remote signals or barrier semaphores. Data moves between devices by JAX's collectives and lax.ppermute only.
A program may use at most 64 MiB of HBM per device.

```python
import math
import jax
import jax.numpy as jnp
from jax import lax

BLK = 512
NBLK = 32
GROUPS = 16


def shard_levels(own_key, extent, pieces, least, largest):
    level, own = 1.0, jax.random.fold_in(own_key, 6)
    for axis_at, shards_of in pieces:
        draws = jnp.exp(jax.random.uniform(jax.random.fold_in(own, axis_at), (shards_of,), jnp.float32, least / len(pieces), largest / len(pieces)))
        level = level * jnp.repeat(draws, extent[axis_at] // shards_of).reshape([-1 if axis == axis_at else 1 for axis in range(len(extent))])
    return level


def gaussian(rng, shape, width, limit, shards=(), dtype=jnp.bfloat16):
    entries = jax.random.normal(rng, shape, jnp.float32) * width
    if len(shards) > 0:
        entries = shard_levels(rng, shape, shards, -0.22, 0.18) * entries
    return jnp.clip(entries, min=-limit, max=limit).astype(dtype)


def setup_inputs(seed: int = 0) -> dict:
    streams_of = jax.random.split(jax.random.key(seed), 11)
    return {
        "up_partials": gaussian(streams_of[0], (GROUPS, NBLK, BLK, BLK), 0.25, 1.5, ((0, 16), (2, 32))),
        "down_partials": gaussian(streams_of[1], (GROUPS, NBLK, BLK, BLK), 0.25, 1.5, ((0, 16), (2, 32))),
        "up_left": gaussian(streams_of[2], (NBLK, BLK, BLK), BLK ** -0.5, 0.25, ((0, 32),)),
        "up_right": gaussian(streams_of[3], (NBLK, BLK, BLK), BLK ** -0.5, 0.25, ((0, 32),)),
        "down_left": gaussian(streams_of[4], (NBLK, BLK, BLK), BLK ** -0.5, 0.25, ((0, 32),)),
        "down_right": gaussian(streams_of[5], (NBLK, BLK, BLK), BLK ** -0.5, 0.25, ((0, 32),)),
        "up_first": gaussian(streams_of[6], (NBLK, BLK, BLK), 1.0, 4.0, ((0, 32), (1, 16)), jnp.float32),
        "up_second": jnp.clip(jnp.exp(math.log(2.0) - 2.3025851 * jax.random.uniform(streams_of[7], (NBLK, BLK, BLK), jnp.float32) ** shard_levels(streams_of[7], (NBLK, BLK, BLK), ((0, 32), (1, 16)), -0.2, 0.2)), 0.2, 2.0),
        "down_first": gaussian(streams_of[8], (NBLK, BLK, BLK), 1.0, 4.0, ((0, 32), (1, 16)), jnp.float32),
        "down_second": jnp.clip(jnp.exp(math.log(2.0) - 2.3025851 * jax.random.uniform(streams_of[9], (NBLK, BLK, BLK), jnp.float32) ** shard_levels(streams_of[9], (NBLK, BLK, BLK), ((0, 32), (1, 16)), -0.2, 0.2)), 0.2, 2.0),
    }


HIGH = lax.Precision.HIGHEST
CORR_FIRST = 1.0 - 0.9 ** 50 * 0.9 ** 50
CORR_SECOND = 1.0 - 0.95 ** 50 * 0.95 ** 50

def one_projection(partials, left, right, first, second):
    grad = lax.optimization_barrier(jnp.sum(partials.astype(jnp.float32), axis=0))
    left_f = left.astype(jnp.float32)
    right_f = right.astype(jnp.float32)
    half = jnp.einsum('bpr,bpq->brq', left_f, grad, precision=HIGH)
    rotated = jnp.einsum('brq,bqc->brc', half, right_f, precision=HIGH)
    first_new = 0.9 * first + 0.1 * rotated
    second_new = 0.95 * second + 0.05 * rotated * rotated
    direction = (first_new / CORR_FIRST / (jnp.sqrt(second_new / CORR_SECOND) + 1e-08)).astype(jnp.bfloat16)
    direction = lax.optimization_barrier(direction)
    middle = jnp.einsum('brq,bcq->brc', direction.astype(jnp.float32), right_f, precision=HIGH)
    update = jnp.einsum('bpr,brc->bpc', left_f, middle, precision=HIGH).astype(jnp.bfloat16)
    return (first_new, second_new, update)

def reference(up_partials, down_partials, up_left, up_right, down_left, down_right, up_first, up_second, down_first, down_second):
    up_m, up_v, up_u = one_projection(up_partials, up_left, up_right, up_first, up_second)
    dn_m, dn_v, dn_u = one_projection(down_partials, down_left, down_right, down_first, down_second)
    return (up_m, up_v, dn_m, dn_v, up_u, dn_u)
```

```python
import jax
import jax.numpy as jnp
from jax import lax
from jax.sharding import PartitionSpec as P

CORR_FIRST = 1.0 - 0.9**50 * 0.9**50
CORR_SECOND = 1.0 - 0.95**50 * 0.95**50
BF = jnp.bfloat16
F32 = jnp.float32


def exchange(x, axis):
    return lax.all_to_all(x, axis, 0, 0, tiled=True)


def moments(rotated, first, second):
    first_new = 0.9 * first + 0.1 * rotated
    second_new = 0.95 * second + 0.05 * rotated * rotated
    direction = first_new / CORR_FIRST / (jnp.sqrt(second_new / CORR_SECOND) + 1e-08)
    return first_new, second_new, direction.astype(BF)


def per_device(
    up_partials,
    down_partials,
    up_left,
    up_right,
    down_left,
    down_right,
    up_first,
    up_second,
    down_first,
    down_second,
):
    me = lax.axis_index("dp")
    proj, part = me % 2, (me // 2) % 2

    both = jnp.stack([up_partials[0], down_partials[0]])
    chunks = both.reshape(2, 32, 2, 8, 4, 128).transpose(4, 2, 0, 1, 3, 5).reshape(16, 32, 8, 128)
    summed = jnp.sum(exchange(chunks, "dp").astype(F32), axis=0).astype(BF)
    grad = exchange(summed, "mp").reshape(256, 128)

    left = jnp.where(proj == 0, up_left[0], down_left[0]).reshape(32, 2, 8, 512)
    left = lax.dynamic_index_in_dim(left, part, 1, keepdims=False).reshape(256, 512)
    half = jnp.einsum("pr,pq->rq", left, grad, preferred_element_type=F32)
    half = exchange(half.astype(BF).reshape(16, 32, 128), "dp")
    half = jnp.sum(half.reshape(4, 2, 2, 32, 128).astype(F32), axis=1).astype(BF)

    outs, mids = [], []
    for k, (right, first, second) in enumerate(
        ((up_right, up_first, up_second), (down_right, down_first, down_second))
    ):
        rows = half[:, k].transpose(1, 0, 2).reshape(32, 512)
        rotated = jnp.einsum("rq,qc->rc", rows, right[0], preferred_element_type=F32)
        first_new, second_new, direction = moments(rotated, first[0], second[0])
        outs += [first_new[None], second_new[None]]
        mid = jnp.einsum("rq,cq->rc", direction, right[0], preferred_element_type=F32)
        mids.append(mid.astype(BF).reshape(32, 16, 32).transpose(1, 0, 2))
    mid = exchange(jnp.concatenate(mids, axis=2), "dp").reshape(512, 64)

    zero = jnp.zeros((512, 32), BF)
    up_mid, down_mid = mid[:, :32], mid[:, 32:]
    packed = 0.0
    for part_at in range(2):
        for k, (own, block) in enumerate(((up_mid, up_left), (down_mid, down_left))):
            at = 2 * part_at + k
            lanes = jnp.concatenate([own if at == j else zero for j in range(4)], axis=1)
            rows = block[0].reshape(32, 2, 8, 512)[:, part_at].reshape(256, 512)
            packed = packed + jnp.einsum("pr,rc->pc", rows, lanes, preferred_element_type=F32)
    packed = exchange(packed.astype(BF).reshape(32, 8, 128), "mp").reshape(32, 8, 2, 2, 32)
    packed = packed.transpose(3, 0, 2, 1, 4).reshape(2, 32, 16, 32)
    return (*outs, packed[0], packed[1])


def solution(mesh):
    blocks, rows = P("mp", None, None), P("mp", "dp", None)
    partials, update = P("dp", None, "mp", None), P(None, "mp", "dp")
    return jax.shard_map(
        per_device,
        mesh=mesh,
        in_specs=(partials, partials, blocks, blocks, blocks, blocks, rows, rows, rows, rows),
        out_specs=(rows, rows, rows, rows, update, update),
        check_vma=False,
    )
```

```python
import jax
import jax.numpy as jnp
from jax import lax
from jax.experimental import pallas as pl
from jax.experimental.pallas import tpu as pltpu
from jax.sharding import Mesh
from jax.sharding import PartitionSpec as P

CORR_FIRST = 1.0 - 0.9**50 * 0.9**50
CORR_SECOND = 1.0 - 0.95**50 * 0.95**50
BF = jnp.bfloat16
F32 = jnp.float32
DP = ("x", "y", "core")
PARAMS = pltpu.CompilerParams(vmem_limit_bytes=16 * 2**20)


def exchange(x, axis):
    return lax.all_to_all(x, axis, 0, 0, tiled=True)


def call(kernel, out_shape, *args):
    return pl.pallas_call(kernel, out_shape=out_shape, compiler_params=PARAMS)(*args)


def chunk_kernel(up_ref, down_ref, got_ref, out_ref):
    def chunks(own_ref):
        for at in range(4):
            lanes = pl.ds(128 * at, 128)
            total = own_ref[0, :, :, lanes].astype(F32) + got_ref[:, :, lanes].astype(F32)
            total = total.reshape(16, 2, 2, 8, 128)
            for half in range(2):
                out_ref[2 * at + half] = total[:, :, half].reshape(16, 16, 128).astype(BF)

    core = lax.axis_index("core")

    @pl.when(core == 0)
    def _():
        chunks(up_ref)

    @pl.when(core == 1)
    def _():
        chunks(down_ref)


def middle_kernel(
    half_ref,
    up_right,
    down_right,
    up_first,
    up_second,
    down_first,
    down_second,
    up_first_new,
    up_second_new,
    down_first_new,
    down_second_new,
    mid_ref,
):
    mids = []
    for k, (right, first, second, first_out, second_out) in enumerate(
        (
            (up_right, up_first, up_second, up_first_new, up_second_new),
            (down_right, down_first, down_second, down_first_new, down_second_new),
        )
    ):
        tiles = [
            (half_ref[4 * at + k].astype(F32) + half_ref[4 * at + 2 + k].astype(F32)).astype(BF)
            for at in range(4)
        ]
        rows = jnp.concatenate(tiles, axis=1)
        rotated = jnp.dot(rows, right[0], preferred_element_type=F32)
        first_new = 0.9 * first[0] + 0.1 * rotated
        second_new = 0.95 * second[0] + 0.05 * rotated * rotated
        first_out[0] = first_new
        second_out[0] = second_new
        direction = first_new / CORR_FIRST / (jnp.sqrt(second_new / CORR_SECOND) + 1e-08)
        mids.append(
            lax.dot_general(
                direction.astype(BF),
                right[0],
                (((1,), (1,)), ((), ())),
                preferred_element_type=F32,
            )
        )
    lane = lax.broadcasted_iota(jnp.int32, (16, 128), 1)
    for at in range(4):
        pieces = [
            mids[k][16 * rh : 16 * rh + 16, 128 * at : 128 * at + 128]
            for rh in range(2)
            for k in range(2)
        ]
        for w in range(4):
            rolled = [
                piece if g == w else pltpu.roll(piece, (32 * (g - w)) % 128, 1)
                for g, piece in enumerate(pieces)
            ]
            packed = jnp.where(
                lane < 64,
                jnp.where(lane < 32, rolled[0], rolled[1]),
                jnp.where(lane < 96, rolled[2], rolled[3]),
            )
            mid_ref[4 * at + w] = packed.astype(BF)


def back_kernel(mid_ref, up_left, down_left, out_ref):
    mid = mid_ref[...].astype(F32)
    other = pltpu.roll(mid.reshape(256, 128), 64, 1).reshape(16, 16, 128)
    mid = jnp.stack([mid, other], axis=1).reshape(512, 128).astype(BF)
    up = jnp.dot(up_left[0], mid, preferred_element_type=F32)
    down = jnp.dot(down_left[0], mid, preferred_element_type=F32)
    lane = lax.broadcasted_iota(jnp.int32, (512, 128), 1)
    both = jnp.where(lane < 32, up, down).reshape(32, 2, 8, 128)
    top = both[:, 0].reshape(256, 128)
    low = pltpu.roll(both[:, 1].reshape(256, 128), 64, 1)
    lane = lax.broadcasted_iota(jnp.int32, (256, 128), 1)
    out_ref[...] = jnp.where(lane < 64, top, low).reshape(16, 16, 128).astype(BF)


def unpack_kernel(got_ref, up_ref, down_ref):
    got = got_ref[...].astype(F32).reshape(256, 128)
    low = pltpu.roll(got, 64, 1)
    rows = jnp.stack([got.reshape(32, 8, 128), low.reshape(32, 8, 128)], axis=1)
    rows = rows.reshape(512, 128)
    up_ref[...] = rows[:, :32].reshape(32, 16, 32).astype(BF)
    down_ref[...] = pltpu.roll(rows, 96, 1)[:, :32].reshape(32, 16, 32).astype(BF)


def per_device(
    up_partials,
    down_partials,
    up_left,
    up_right,
    down_left,
    down_right,
    up_first,
    up_second,
    down_first,
    down_second,
):
    core, part = lax.axis_index("core"), lax.axis_index("y")

    sent = jnp.where(core == 0, down_partials[0], up_partials[0])
    got = lax.ppermute(sent, "core", [(0, 1), (1, 0)])
    chunks = call(
        chunk_kernel,
        jax.ShapeDtypeStruct((8, 16, 16, 128), BF),
        up_partials,
        down_partials,
        got,
    )
    summed = jnp.sum(exchange(chunks, ("x", "y")).astype(F32), axis=0).astype(BF)
    grad = exchange(summed.reshape(32, 8, 128), "mp").reshape(256, 128)

    left = jnp.where(core == 0, up_left[0], down_left[0]).reshape(32, 2, 8, 512)
    left = lax.dynamic_index_in_dim(left, part, 1, keepdims=False).reshape(256, 512)
    half = jnp.einsum("pr,pq->rq", left, grad, preferred_element_type=F32)
    half = exchange(half.astype(BF).reshape(16, 32, 128), DP)

    rows = jax.ShapeDtypeStruct((1, 32, 512), F32)
    *moments, mid = call(
        middle_kernel,
        [rows] * 4 + [jax.ShapeDtypeStruct((16, 16, 128), BF)],
        half,
        up_right,
        down_right,
        up_first,
        up_second,
        down_first,
        down_second,
    )
    mid = exchange(mid, DP)
    packed = call(
        back_kernel, jax.ShapeDtypeStruct((16, 16, 128), BF), mid, up_left, down_left
    )
    packed = exchange(packed.reshape(32, 8, 128), "mp").reshape(16, 16, 128)
    updates = call(unpack_kernel, [jax.ShapeDtypeStruct((32, 16, 32), BF)] * 2, packed)
    return (*moments, *updates)


def solution(mesh):
    mesh = Mesh(mesh.devices.reshape(4, 2, 2, 32), ("x", "y", "core", "mp"))
    blocks, rows = P("mp", None, None), P("mp", DP, None)
    partials, update = P(DP, None, "mp", None), P(None, "mp", DP)
    return jax.shard_map(
        per_device,
        mesh=mesh,
        in_specs=(partials, partials, blocks, blocks, blocks, blocks, rows, rows, rows, rows),
        out_specs=(rows, rows, rows, rows, update, update),
        check_vma=False,
    )
```

```python
import jax
import jax.numpy as jnp
from jax import lax
from jax.experimental import pallas as pl
from jax.experimental.pallas import tpu as pltpu
from jax.sharding import Mesh
from jax.sharding import PartitionSpec as P

CORR_FIRST = 1.0 - 0.9**50 * 0.9**50
CORR_SECOND = 1.0 - 0.95**50 * 0.95**50
BF = jnp.bfloat16
F32 = jnp.float32
DP = ("x", "y", "core")
PARAMS = pltpu.CompilerParams(vmem_limit_bytes=16 * 2**20)


def exchange(x, axis):
    return lax.all_to_all(x, axis, 0, 0, tiled=True)


def call(kernel, out_shape, *args):
    return pl.pallas_call(kernel, out_shape=out_shape, compiler_params=PARAMS)(*args)


def chunk_kernel(up_ref, down_ref, got_ref, out_ref):
    def chunks(own_ref):
        for at in range(4):
            lanes = pl.ds(128 * at, 128)
            total = own_ref[0, :, :, lanes].astype(F32) + got_ref[:, :, lanes].astype(F32)
            total = total.reshape(16, 2, 2, 8, 128)
            for half in range(2):
                out_ref[2 * at + half] = total[:, :, half].reshape(16, 16, 128).astype(BF)

    core = lax.axis_index("core")

    @pl.when(core == 0)
    def _():
        chunks(up_ref)

    @pl.when(core == 1)
    def _():
        chunks(down_ref)


def middle_kernel(
    half_ref,
    up_right,
    down_right,
    up_first,
    up_second,
    down_first,
    down_second,
    up_first_new,
    up_second_new,
    down_first_new,
    down_second_new,
    mid_ref,
):
    mids = []
    for k, (right, first, second, first_out, second_out) in enumerate(
        (
            (up_right, up_first, up_second, up_first_new, up_second_new),
            (down_right, down_first, down_second, down_first_new, down_second_new),
        )
    ):
        tiles = [
            (half_ref[4 * at + k].astype(F32) + half_ref[4 * at + 2 + k].astype(F32)).astype(BF)
            for at in range(4)
        ]
        rows = jnp.concatenate(tiles, axis=1)
        rotated = jnp.dot(rows, right[0], preferred_element_type=F32)
        first_new = 0.9 * first[0] + 0.1 * rotated
        second_new = 0.95 * second[0] + 0.05 * rotated * rotated
        first_out[0] = first_new
        second_out[0] = second_new
        direction = first_new / CORR_FIRST / (jnp.sqrt(second_new / CORR_SECOND) + 1e-08)
        mids.append(
            lax.dot_general(
                direction.astype(BF),
                right[0],
                (((1,), (1,)), ((), ())),
                preferred_element_type=F32,
            )
        )
    lane = lax.broadcasted_iota(jnp.int32, (16, 128), 1)
    for at in range(4):
        pieces = [
            mids[k][16 * rh : 16 * rh + 16, 128 * at : 128 * at + 128]
            for rh in range(2)
            for k in range(2)
        ]
        for w in range(4):
            rolled = [
                piece if g == w else pltpu.roll(piece, (32 * (g - w)) % 128, 1)
                for g, piece in enumerate(pieces)
            ]
            packed = jnp.where(
                lane < 64,
                jnp.where(lane < 32, rolled[0], rolled[1]),
                jnp.where(lane < 96, rolled[2], rolled[3]),
            )
            mid_ref[4 * at + w] = packed.astype(BF)


def back_kernel(mid_ref, up_left, down_left, out_ref):
    mid = mid_ref[...].astype(F32)
    other = pltpu.roll(mid.reshape(256, 128), 64, 1).reshape(16, 16, 128)
    mid = jnp.stack([mid, other], axis=1).reshape(512, 128).astype(BF)
    up = jnp.dot(up_left[0], mid, preferred_element_type=F32)
    down = jnp.dot(down_left[0], mid, preferred_element_type=F32)
    lane = lax.broadcasted_iota(jnp.int32, (512, 128), 1)
    both = jnp.where(lane < 32, up, down).reshape(32, 2, 8, 128)
    top = both[:, 0].reshape(256, 128)
    low = pltpu.roll(both[:, 1].reshape(256, 128), 64, 1)
    lane = lax.broadcasted_iota(jnp.int32, (256, 128), 1)
    out_ref[...] = jnp.where(lane < 64, top, low).reshape(16, 16, 128).astype(BF)


def unpack_kernel(got_ref, up_ref, down_ref):
    got = got_ref[...].astype(F32).reshape(256, 128)
    low = pltpu.roll(got, 64, 1)
    rows = jnp.stack([got.reshape(32, 8, 128), low.reshape(32, 8, 128)], axis=1)
    rows = rows.reshape(512, 128)
    up_ref[...] = rows[:, :32].reshape(32, 16, 32).astype(BF)
    down_ref[...] = pltpu.roll(rows, 96, 1)[:, :32].reshape(32, 16, 32).astype(BF)


def per_device(
    up_partials,
    down_partials,
    up_left,
    up_right,
    down_left,
    down_right,
    up_first,
    up_second,
    down_first,
    down_second,
):
    core, part = lax.axis_index("core"), lax.axis_index("y")

    sent = jnp.where(core == 0, down_partials[0], up_partials[0])
    got = lax.ppermute(sent, "core", [(0, 1), (1, 0)])
    left = jnp.where(core == 0, up_left[0], down_left[0]).reshape(32, 2, 8, 512)
    left = lax.dynamic_index_in_dim(left, part, 1, keepdims=False).reshape(256, 512)
    got, left = lax.optimization_barrier((got, left))
    chunks = call(
        chunk_kernel,
        jax.ShapeDtypeStruct((8, 16, 16, 128), BF),
        up_partials,
        down_partials,
        got,
    )
    summed = jnp.sum(exchange(chunks, ("x", "y")).astype(F32), axis=0).astype(BF)
    grad = exchange(summed.reshape(32, 8, 128), "mp").reshape(256, 128)
    half = jnp.einsum("pr,pq->rq", left, grad, preferred_element_type=F32)
    half = exchange(half.astype(BF).reshape(16, 32, 128), DP)

    rows = jax.ShapeDtypeStruct((1, 32, 512), F32)
    *moments, mid = call(
        middle_kernel,
        [rows] * 4 + [jax.ShapeDtypeStruct((16, 16, 128), BF)],
        half,
        up_right,
        down_right,
        up_first,
        up_second,
        down_first,
        down_second,
    )
    mid = exchange(mid, DP)
    packed = call(
        back_kernel, jax.ShapeDtypeStruct((16, 16, 128), BF), mid, up_left, down_left
    )
    packed = exchange(packed.reshape(32, 8, 128), "mp").reshape(16, 16, 128)
    updates = call(unpack_kernel, [jax.ShapeDtypeStruct((32, 16, 32), BF)] * 2, packed)
    return (*moments, *updates)


def solution(mesh):
    mesh = Mesh(mesh.devices.reshape(4, 2, 2, 32), ("x", "y", "core", "mp"))
    blocks, rows = P("mp", None, None), P("mp", DP, None)
    partials, update = P(DP, None, "mp", None), P(None, "mp", DP)
    return jax.shard_map(
        per_device,
        mesh=mesh,
        in_specs=(partials, partials, blocks, blocks, blocks, blocks, rows, rows, rows, rows),
        out_specs=(rows, rows, rows, rows, update, update),
        check_vma=False,
    )
```

```python
import jax
import jax.numpy as jnp
from jax import lax
from jax.experimental import pallas as pl
from jax.experimental.pallas import tpu as pltpu
from jax.sharding import Mesh
from jax.sharding import PartitionSpec as P

CORR_FIRST = 1.0 - 0.9**50 * 0.9**50
CORR_SECOND = 1.0 - 0.95**50 * 0.95**50
BF = jnp.bfloat16
F32 = jnp.float32
DP = ("x", "y", "core")
PARAMS = pltpu.CompilerParams(vmem_limit_bytes=16 * 2**20)


def exchange(x, axis):
    return lax.all_to_all(x, axis, 0, 0, tiled=True)


def call(kernel, out_shape, *args):
    return pl.pallas_call(kernel, out_shape=out_shape, compiler_params=PARAMS)(*args)


def chunk_kernel(up_ref, down_ref, got_ref, out_ref):
    def chunks(own_ref):
        for at in range(4):
            lanes = pl.ds(128 * at, 128)
            total = own_ref[0, :, :, lanes].astype(F32) + got_ref[:, :, lanes].astype(F32)
            total = total.reshape(16, 2, 2, 8, 128)
            for half in range(2):
                out_ref[2 * at + half] = total[:, :, half].reshape(16, 16, 128).astype(BF)

    core = lax.axis_index("core")

    @pl.when(core == 0)
    def _():
        chunks(up_ref)

    @pl.when(core == 1)
    def _():
        chunks(down_ref)


def middle_kernel(
    half_ref,
    up_right,
    down_right,
    up_first,
    up_second,
    down_first,
    down_second,
    up_first_new,
    up_second_new,
    down_first_new,
    down_second_new,
    mid_ref,
):
    mids = []
    for k, (right, first, second, first_out, second_out) in enumerate(
        (
            (up_right, up_first, up_second, up_first_new, up_second_new),
            (down_right, down_first, down_second, down_first_new, down_second_new),
        )
    ):
        tiles = [
            (half_ref[4 * at + k].astype(F32) + half_ref[4 * at + 2 + k].astype(F32)).astype(BF)
            for at in range(4)
        ]
        rows = jnp.concatenate(tiles, axis=1)
        rotated = jnp.dot(rows, right[0], preferred_element_type=F32)
        first_new = 0.9 * first[0] + 0.1 * rotated
        second_new = 0.95 * second[0] + 0.05 * rotated * rotated
        first_out[0] = first_new
        second_out[0] = second_new
        direction = first_new / CORR_FIRST / (jnp.sqrt(second_new / CORR_SECOND) + 1e-08)
        mids.append(
            lax.dot_general(
                direction.astype(BF),
                right[0],
                (((1,), (1,)), ((), ())),
                preferred_element_type=F32,
            )
        )
    lane = lax.broadcasted_iota(jnp.int32, (16, 128), 1)
    for at in range(4):
        pieces = [
            mids[k][16 * rh : 16 * rh + 16, 128 * at : 128 * at + 128]
            for rh in range(2)
            for k in range(2)
        ]
        for w in range(4):
            rolled = [
                piece if g == w else pltpu.roll(piece, (32 * (g - w)) % 128, 1)
                for g, piece in enumerate(pieces)
            ]
            packed = jnp.where(
                lane < 64,
                jnp.where(lane < 32, rolled[0], rolled[1]),
                jnp.where(lane < 96, rolled[2], rolled[3]),
            )
            mid_ref[4 * at + w] = packed.astype(BF)


def back_kernel(mid_ref, up_left, down_left, out_ref):
    mid = mid_ref[...].astype(F32)
    other = pltpu.roll(mid.reshape(256, 128), 64, 1).reshape(16, 16, 128)
    mid = jnp.stack([mid, other], axis=1).reshape(512, 128).astype(BF)
    up = jnp.dot(up_left[0], mid, preferred_element_type=F32)
    down = jnp.dot(down_left[0], mid, preferred_element_type=F32)
    lane = lax.broadcasted_iota(jnp.int32, (512, 128), 1)
    both = jnp.where(lane < 32, up, down).reshape(32, 2, 8, 128)
    top = both[:, 0].reshape(256, 128)
    low = pltpu.roll(both[:, 1].reshape(256, 128), 64, 1)
    lane = lax.broadcasted_iota(jnp.int32, (256, 128), 1)
    out_ref[...] = jnp.where(lane < 64, top, low).reshape(16, 16, 128).astype(BF)


def unpack_kernel(got_ref, *refs):
    *moments, up_ref, down_ref = refs
    for own_ref, out_ref in zip(moments[:4], moments[4:]):
        out_ref[...] = own_ref[...]
    got = got_ref[...].astype(F32).reshape(256, 128)
    low = pltpu.roll(got, 64, 1)
    rows = jnp.stack([got.reshape(32, 8, 128), low.reshape(32, 8, 128)], axis=1)
    rows = rows.reshape(512, 128)
    up_ref[...] = rows[:, :32].reshape(32, 16, 32).astype(BF)
    down_ref[...] = pltpu.roll(rows, 96, 1)[:, :32].reshape(32, 16, 32).astype(BF)


def per_device(
    up_partials,
    down_partials,
    up_left,
    up_right,
    down_left,
    down_right,
    up_first,
    up_second,
    down_first,
    down_second,
):
    core, part = lax.axis_index("core"), lax.axis_index("y")

    sent = jnp.where(core == 0, down_partials[0], up_partials[0])
    got = lax.ppermute(sent, "core", [(0, 1), (1, 0)])
    left = jnp.where(core == 0, up_left[0], down_left[0]).reshape(32, 2, 8, 512)
    left = lax.dynamic_index_in_dim(left, part, 1, keepdims=False).reshape(256, 512)
    got, left = lax.optimization_barrier((got, left))
    chunks = call(
        chunk_kernel,
        jax.ShapeDtypeStruct((8, 16, 16, 128), BF),
        up_partials,
        down_partials,
        got,
    )
    summed = jnp.sum(exchange(chunks, ("x", "y")).astype(F32), axis=0).astype(BF)
    grad = exchange(summed.reshape(32, 8, 128), "mp").reshape(256, 128)
    half = jnp.einsum("pr,pq->rq", left, grad, preferred_element_type=F32)
    half = exchange(half.astype(BF).reshape(16, 32, 128), DP)

    rows = jax.ShapeDtypeStruct((1, 32, 512), F32)
    *moments, mid = call(
        middle_kernel,
        [rows] * 4 + [jax.ShapeDtypeStruct((16, 16, 128), BF)],
        half,
        up_right,
        down_right,
        up_first,
        up_second,
        down_first,
        down_second,
    )
    mid = exchange(mid, DP)
    packed = call(
        back_kernel, jax.ShapeDtypeStruct((16, 16, 128), BF), mid, up_left, down_left
    )
    packed = exchange(packed.reshape(32, 8, 128), "mp").reshape(16, 16, 128)
    update = jax.ShapeDtypeStruct((32, 16, 32), BF)
    return tuple(call(unpack_kernel, [rows] * 4 + [update] * 2, packed, *moments))


def solution(mesh):
    mesh = Mesh(mesh.devices.reshape(4, 2, 2, 32), ("x", "y", "core", "mp"))
    blocks, rows = P("mp", None, None), P("mp", DP, None)
    partials, update = P(DP, None, "mp", None), P(None, "mp", DP)
    return jax.shard_map(
        per_device,
        mesh=mesh,
        in_specs=(partials, partials, blocks, blocks, blocks, blocks, rows, rows, rows, rows),
        out_specs=(rows, rows, rows, rows, update, update),
        check_vma=False,
    )
```

```python
import jax
import jax.numpy as jnp
from jax import lax
from jax.experimental import pallas as pl
from jax.experimental.pallas import tpu as pltpu
from jax.sharding import Mesh
from jax.sharding import PartitionSpec as P

CORR_FIRST = 1.0 - 0.9**50 * 0.9**50
CORR_SECOND = 1.0 - 0.95**50 * 0.95**50
BF = jnp.bfloat16
F32 = jnp.float32
DP = ("x", "y", "core")
MP = ("z", "h")
PARAMS = pltpu.CompilerParams(vmem_limit_bytes=16 * 2**20)


def exchange(x, axis):
    return lax.all_to_all(x, axis, 0, 0, tiled=True)


def call(kernel, out_shape, *args):
    return pl.pallas_call(kernel, out_shape=out_shape, compiler_params=PARAMS)(*args)


def chunk_kernel(up_ref, down_ref, got_ref, out_ref):
    def chunks(own_ref):
        for at in range(4):
            lanes = pl.ds(128 * at, 128)
            total = own_ref[0, :, :, lanes].astype(F32) + got_ref[:, :, lanes].astype(F32)
            total = total.reshape(16, 2, 2, 8, 128)
            for half in range(2):
                for odd in range(2):
                    part = total[:, odd, half].reshape(8, 16, 128)
                    out_ref[8 * odd + 2 * at + 1 * half] = part.astype(BF)

    core = lax.axis_index("core")

    @pl.when(core == 0)
    def _():
        chunks(up_ref)

    @pl.when(core == 1)
    def _():
        chunks(down_ref)


def sum_kernel(got_ref, out_ref):
    sums = []
    for odd in range(2):
        total = 0.0
        for at in range(4):
            for half in range(2):
                total = total + got_ref[8 * odd + 2 * at + 1 * half].astype(F32)
        sums.append(total.reshape(16, 8, 128))
    out_ref[...] = jnp.stack(sums, axis=1).reshape(16, 16, 128).astype(BF)


def middle_kernel(
    half_ref,
    up_right,
    down_right,
    up_first,
    up_second,
    down_first,
    down_second,
    up_first_new,
    up_second_new,
    down_first_new,
    down_second_new,
    mid_ref,
):
    mids = []
    for k, (right, first, second, first_out, second_out) in enumerate(
        (
            (up_right, up_first, up_second, up_first_new, up_second_new),
            (down_right, down_first, down_second, down_first_new, down_second_new),
        )
    ):
        tiles = [
            (half_ref[4 * at + k].astype(F32) + half_ref[4 * at + 2 + k].astype(F32)).astype(BF)
            for at in range(4)
        ]
        rows = jnp.concatenate(tiles, axis=1)
        rotated = jnp.dot(rows, right[0], preferred_element_type=F32)
        first_new = 0.9 * first[0] + 0.1 * rotated
        second_new = 0.95 * second[0] + 0.05 * rotated * rotated
        first_out[0] = first_new
        second_out[0] = second_new
        direction = first_new / CORR_FIRST / (jnp.sqrt(second_new / CORR_SECOND) + 1e-08)
        mids.append(
            lax.dot_general(
                direction.astype(BF),
                right[0],
                (((1,), (1,)), ((), ())),
                preferred_element_type=F32,
            )
        )
    lane = lax.broadcasted_iota(jnp.int32, (16, 128), 1)
    for at in range(4):
        pieces = [
            mids[k][16 * rh : 16 * rh + 16, 128 * at : 128 * at + 128]
            for rh in range(2)
            for k in range(2)
        ]
        for w in range(4):
            rolled = [
                piece if g == w else pltpu.roll(piece, (32 * (g - w)) % 128, 1)
                for g, piece in enumerate(pieces)
            ]
            packed = jnp.where(
                lane < 64,
                jnp.where(lane < 32, rolled[0], rolled[1]),
                jnp.where(lane < 96, rolled[2], rolled[3]),
            )
            mid_ref[4 * at + w] = packed.astype(BF)


def back_kernel(mid_ref, up_left, down_left, out_ref):
    mid = mid_ref[...].astype(F32)
    other = pltpu.roll(mid.reshape(256, 128), 64, 1).reshape(16, 16, 128)
    mid = jnp.stack([mid, other], axis=1).reshape(512, 128).astype(BF)
    up = jnp.dot(up_left[0], mid, preferred_element_type=F32)
    down = jnp.dot(down_left[0], mid, preferred_element_type=F32)
    lane = lax.broadcasted_iota(jnp.int32, (512, 128), 1)
    both = jnp.where(lane < 32, up, down).reshape(32, 2, 8, 128)
    top = both[:, 0].reshape(256, 128)
    low = pltpu.roll(both[:, 1].reshape(256, 128), 64, 1)
    lane = lax.broadcasted_iota(jnp.int32, (256, 128), 1)
    out_ref[...] = jnp.where(lane < 64, top, low).reshape(16, 16, 128).astype(BF)


def unpack_kernel(got_ref, *refs):
    *moments, up_ref, down_ref = refs
    for own_ref, out_ref in zip(moments[:4], moments[4:]):
        out_ref[...] = own_ref[...]
    got = got_ref[...].astype(F32).reshape(256, 128)
    low = pltpu.roll(got, 64, 1)
    rows = jnp.stack([got.reshape(32, 8, 128), low.reshape(32, 8, 128)], axis=1)
    rows = rows.reshape(512, 128)
    up_ref[...] = rows[:, :32].reshape(32, 16, 32).astype(BF)
    down_ref[...] = pltpu.roll(rows, 96, 1)[:, :32].reshape(32, 16, 32).astype(BF)


def per_device(
    up_partials,
    down_partials,
    up_left,
    up_right,
    down_left,
    down_right,
    up_first,
    up_second,
    down_first,
    down_second,
):
    core, part = lax.axis_index("core"), lax.axis_index("y")

    sent = jnp.where(core == 0, down_partials[0], up_partials[0])
    got = lax.ppermute(sent, "core", [(0, 1), (1, 0)])
    left = jnp.where(core == 0, up_left[0], down_left[0]).reshape(32, 2, 8, 512)
    left = lax.dynamic_index_in_dim(left, part, 1, keepdims=False).reshape(256, 512)
    got, left = lax.optimization_barrier((got, left))
    chunks = call(
        chunk_kernel,
        jax.ShapeDtypeStruct((16, 8, 16, 128), BF),
        up_partials,
        down_partials,
        got,
    )
    got = exchange(chunks, ("h", "x", "y"))
    summed = call(sum_kernel, jax.ShapeDtypeStruct((16, 16, 128), BF), got)
    grad = exchange(summed, "z").reshape(256, 128)
    half = jnp.einsum("pr,pq->rq", left, grad, preferred_element_type=F32)
    half = exchange(half.astype(BF).reshape(16, 32, 128), DP)

    rows = jax.ShapeDtypeStruct((1, 32, 512), F32)
    *moments, mid = call(
        middle_kernel,
        [rows] * 4 + [jax.ShapeDtypeStruct((16, 16, 128), BF)],
        half,
        up_right,
        down_right,
        up_first,
        up_second,
        down_first,
        down_second,
    )
    mid = exchange(mid, DP)
    packed = call(
        back_kernel, jax.ShapeDtypeStruct((16, 16, 128), BF), mid, up_left, down_left
    )
    packed = exchange(packed.reshape(32, 8, 128), ("z", "h")).reshape(16, 16, 128)
    update = jax.ShapeDtypeStruct((32, 16, 32), BF)
    return tuple(call(unpack_kernel, [rows] * 4 + [update] * 2, packed, *moments))


def solution(mesh):
    mesh = Mesh(mesh.devices.reshape(4, 2, 2, 16, 2), ("x", "y", "core", "z", "h"))
    blocks, rows = P(MP, None, None), P(MP, DP, None)
    partials, update = P(DP, None, MP, None), P(None, MP, DP)
    return jax.shard_map(
        per_device,
        mesh=mesh,
        in_specs=(partials, partials, blocks, blocks, blocks, blocks, rows, rows, rows, rows),
        out_specs=(rows, rows, rows, rows, update, update),
        check_vma=False,
    )
```

```python
import jax
import jax.numpy as jnp
from jax import lax
from jax.experimental import pallas as pl
from jax.experimental.pallas import tpu as pltpu
from jax.sharding import Mesh
from jax.sharding import PartitionSpec as P

CORR_FIRST = 1.0 - 0.9**50 * 0.9**50
CORR_SECOND = 1.0 - 0.95**50 * 0.95**50
BF = jnp.bfloat16
F32 = jnp.float32
DP = ("x", "y", "core")
MP = ("z", "h")
PARAMS = pltpu.CompilerParams(vmem_limit_bytes=16 * 2**20)


def exchange(x, axis):
    return lax.all_to_all(x, axis, 0, 0, tiled=True)


def call(kernel, out_shape, *args):
    return pl.pallas_call(kernel, out_shape=out_shape, compiler_params=PARAMS)(*args)


def chunk_kernel(up_ref, down_ref, got_ref, out_ref):
    def chunks(own_ref):
        for at in range(4):
            lanes = pl.ds(128 * at, 128)
            total = own_ref[0, :, :, lanes].astype(F32) + got_ref[:, :, lanes].astype(F32)
            total = total.reshape(16, 2, 2, 8, 128)
            for half in range(2):
                for odd in range(2):
                    part = total[:, odd, half].reshape(8, 16, 128)
                    out_ref[8 * odd + 2 * at + 1 * half] = part.astype(BF)

    core = lax.axis_index("core")

    @pl.when(core == 0)
    def _():
        chunks(up_ref)

    @pl.when(core == 1)
    def _():
        chunks(down_ref)


def sum_kernel(got_ref, out_ref):
    sums = []
    for odd in range(2):
        total = 0.0
        for at in range(4):
            for half in range(2):
                total = total + got_ref[8 * odd + 2 * at + 1 * half].astype(F32)
        sums.append(total.reshape(16, 8, 128))
    out_ref[...] = jnp.stack(sums, axis=1).reshape(16, 16, 128).astype(BF)


def middle_kernel(
    half_ref,
    up_right,
    down_right,
    up_first,
    up_second,
    down_first,
    down_second,
    up_first_new,
    up_second_new,
    down_first_new,
    down_second_new,
    mid_ref,
):
    sides = (
        (up_right, up_first, up_second, up_first_new, up_second_new),
        (down_right, down_first, down_second, down_first_new, down_second_new),
    )
    rotated = []
    for k in range(2):
        tiles = [
            (half_ref[4 * at + k].astype(F32) + half_ref[4 * at + 2 + k].astype(F32)).astype(BF)
            for at in range(4)
        ]
        rows = jnp.concatenate(tiles, axis=1)
        rotated.append(jnp.dot(rows, sides[k][0][0], preferred_element_type=F32))
    directions = []
    for k in range(2):
        _, first, second, first_out, second_out = sides[k]
        first_new = 0.9 * first[0] + 0.1 * rotated[k]
        second_new = 0.95 * second[0] + 0.05 * rotated[k] * rotated[k]
        first_out[0] = first_new
        second_out[0] = second_new
        direction = first_new / CORR_FIRST / (jnp.sqrt(second_new / CORR_SECOND) + 1e-08)
        directions.append(direction.astype(BF))
    mids = [
        lax.dot_general(
            directions[k],
            sides[k][0][0],
            (((1,), (1,)), ((), ())),
            preferred_element_type=F32,
        )
        for k in range(2)
    ]
    lane = lax.broadcasted_iota(jnp.int32, (16, 128), 1)
    for at in range(4):
        pieces = [
            mids[k][16 * rh : 16 * rh + 16, 128 * at : 128 * at + 128]
            for rh in range(2)
            for k in range(2)
        ]
        for w in range(4):
            rolled = [
                piece if g == w else pltpu.roll(piece, (32 * (g - w)) % 128, 1)
                for g, piece in enumerate(pieces)
            ]
            packed = jnp.where(
                lane < 64,
                jnp.where(lane < 32, rolled[0], rolled[1]),
                jnp.where(lane < 96, rolled[2], rolled[3]),
            )
            mid_ref[4 * at + w] = packed.astype(BF)


def back_kernel(mid_ref, up_left, down_left, out_ref):
    mid = mid_ref[...].astype(F32)
    other = pltpu.roll(mid.reshape(256, 128), 64, 1).reshape(16, 16, 128)
    mid = jnp.stack([mid, other], axis=1).reshape(512, 128).astype(BF)
    up = jnp.dot(up_left[0], mid, preferred_element_type=F32)
    down = jnp.dot(down_left[0], mid, preferred_element_type=F32)
    lane = lax.broadcasted_iota(jnp.int32, (512, 128), 1)
    both = jnp.where(lane < 32, up, down).reshape(32, 2, 8, 128)
    top = both[:, 0].reshape(256, 128)
    low = pltpu.roll(both[:, 1].reshape(256, 128), 64, 1)
    lane = lax.broadcasted_iota(jnp.int32, (256, 128), 1)
    out_ref[...] = jnp.where(lane < 64, top, low).reshape(16, 16, 128).astype(BF)


def unpack_kernel(got_ref, *refs):
    *moments, up_ref, down_ref = refs
    for own_ref, out_ref in zip(moments[:4], moments[4:]):
        out_ref[...] = own_ref[...]
    got = got_ref[...].astype(F32).reshape(256, 128)
    low = pltpu.roll(got, 64, 1)
    rows = jnp.stack([got.reshape(32, 8, 128), low.reshape(32, 8, 128)], axis=1)
    rows = rows.reshape(512, 128)
    up_ref[...] = rows[:, :32].reshape(32, 16, 32).astype(BF)
    down_ref[...] = pltpu.roll(rows, 96, 1)[:, :32].reshape(32, 16, 32).astype(BF)


def per_device(
    up_partials,
    down_partials,
    up_left,
    up_right,
    down_left,
    down_right,
    up_first,
    up_second,
    down_first,
    down_second,
):
    core, part = lax.axis_index("core"), lax.axis_index("y")

    sent = jnp.where(core == 0, down_partials[0], up_partials[0])
    got = lax.ppermute(sent, "core", [(0, 1), (1, 0)])
    left = jnp.where(core == 0, up_left[0], down_left[0]).reshape(32, 2, 8, 512)
    left = lax.dynamic_index_in_dim(left, part, 1, keepdims=False).reshape(256, 512)
    got, left = lax.optimization_barrier((got, left))
    chunks = call(
        chunk_kernel,
        jax.ShapeDtypeStruct((16, 8, 16, 128), BF),
        up_partials,
        down_partials,
        got,
    )
    got = exchange(chunks, ("h", "x", "y"))
    summed = call(sum_kernel, jax.ShapeDtypeStruct((16, 16, 128), BF), got)
    grad = exchange(summed, "z").reshape(256, 128)
    half = jnp.einsum("pr,pq->rq", left, grad, preferred_element_type=F32)
    half = exchange(half.astype(BF).reshape(16, 32, 128), DP)

    rows = jax.ShapeDtypeStruct((1, 32, 512), F32)
    *moments, mid = call(
        middle_kernel,
        [rows] * 4 + [jax.ShapeDtypeStruct((16, 16, 128), BF)],
        half,
        up_right,
        down_right,
        up_first,
        up_second,
        down_first,
        down_second,
    )
    mid = exchange(mid, DP)
    packed = call(
        back_kernel, jax.ShapeDtypeStruct((16, 16, 128), BF), mid, up_left, down_left
    )
    packed = exchange(packed.reshape(32, 8, 128), ("z", "h")).reshape(16, 16, 128)
    update = jax.ShapeDtypeStruct((32, 16, 32), BF)
    return tuple(call(unpack_kernel, [rows] * 4 + [update] * 2, packed, *moments))


def solution(mesh):
    mesh = Mesh(mesh.devices.reshape(4, 2, 2, 16, 2), ("x", "y", "core", "z", "h"))
    blocks, rows = P(MP, None, None), P(MP, DP, None)
    partials, update = P(DP, None, MP, None), P(None, MP, DP)
    return jax.shard_map(
        per_device,
        mesh=mesh,
        in_specs=(partials, partials, blocks, blocks, blocks, blocks, rows, rows, rows, rows),
        out_specs=(rows, rows, rows, rows, update, update),
        check_vma=False,
    )
```

```python
import jax
import jax.numpy as jnp
from jax import lax
from jax.experimental import pallas as pl
from jax.experimental.pallas import tpu as pltpu
from jax.sharding import Mesh
from jax.sharding import PartitionSpec as P

CORR_FIRST = 1.0 - 0.9**50 * 0.9**50
CORR_SECOND = 1.0 - 0.95**50 * 0.95**50
BF = jnp.bfloat16
F32 = jnp.float32
DP = ("x", "y", "core")
MP = ("far", "near", "h")
PARAMS = pltpu.CompilerParams(vmem_limit_bytes=16 * 2**20)


def exchange(x, axis):
    return lax.all_to_all(x, axis, 0, 0, tiled=True)


def call(kernel, out_shape, *args):
    return pl.pallas_call(kernel, out_shape=out_shape, compiler_params=PARAMS)(*args)


def chunk_kernel(up_ref, down_ref, got_ref, out_ref):
    def chunks(own_ref):
        for at in range(4):
            lanes = pl.ds(128 * at, 128)
            total = own_ref[0, :, :, lanes].astype(F32) + got_ref[:, :, lanes].astype(F32)
            total = total.reshape(16, 2, 2, 8, 128)
            for half in range(2):
                for odd in range(2):
                    part = total[:, odd, half].reshape(8, 16, 128)
                    out_ref[8 * odd + 2 * at + 1 * half] = part.astype(BF)

    core = lax.axis_index("core")

    @pl.when(core == 0)
    def _():
        chunks(up_ref)

    @pl.when(core == 1)
    def _():
        chunks(down_ref)


def sum_kernel(got_ref, out_ref):
    sums = []
    for odd in range(2):
        total = 0.0
        for at in range(4):
            for half in range(2):
                total = total + got_ref[8 * odd + 2 * at + 1 * half].astype(F32)
        sums.append(total.reshape(16, 8, 128))
    out = jnp.stack(sums, axis=1).reshape(2, 8, 16, 128)
    out = jnp.stack([out[:, near] for near in range(8)])
    out_ref[...] = out.reshape(16, 16, 128).astype(BF)


def middle_kernel(
    half_ref,
    up_right,
    down_right,
    up_first,
    up_second,
    down_first,
    down_second,
    up_first_new,
    up_second_new,
    down_first_new,
    down_second_new,
    mid_ref,
):
    sides = (
        (up_right, up_first, up_second, up_first_new, up_second_new),
        (down_right, down_first, down_second, down_first_new, down_second_new),
    )
    rotated = []
    for k in range(2):
        tiles = [
            (half_ref[4 * at + k].astype(F32) + half_ref[4 * at + 2 + k].astype(F32)).astype(BF)
            for at in range(4)
        ]
        rows = jnp.concatenate(tiles, axis=1)
        rotated.append(jnp.dot(rows, sides[k][0][0], preferred_element_type=F32))
    directions = []
    for k in range(2):
        _, first, second, first_out, second_out = sides[k]
        first_new = 0.9 * first[0] + 0.1 * rotated[k]
        second_new = 0.95 * second[0] + 0.05 * rotated[k] * rotated[k]
        first_out[0] = first_new
        second_out[0] = second_new
        direction = first_new / CORR_FIRST / (jnp.sqrt(second_new / CORR_SECOND) + 1e-08)
        directions.append(direction.astype(BF))
    mids = [
        lax.dot_general(
            directions[k],
            sides[k][0][0],
            (((1,), (1,)), ((), ())),
            preferred_element_type=F32,
        )
        for k in range(2)
    ]
    lane = lax.broadcasted_iota(jnp.int32, (16, 128), 1)
    for at in range(4):
        pieces = [
            mids[k][16 * rh : 16 * rh + 16, 128 * at : 128 * at + 128]
            for rh in range(2)
            for k in range(2)
        ]
        for w in range(4):
            rolled = [
                piece if g == w else pltpu.roll(piece, (32 * (g - w)) % 128, 1)
                for g, piece in enumerate(pieces)
            ]
            packed = jnp.where(
                lane < 64,
                jnp.where(lane < 32, rolled[0], rolled[1]),
                jnp.where(lane < 96, rolled[2], rolled[3]),
            )
            mid_ref[4 * at + w] = packed.astype(BF)


def back_kernel(mid_ref, up_left, down_left, out_ref):
    mid = mid_ref[...].astype(F32)
    other = pltpu.roll(mid.reshape(256, 128), 64, 1).reshape(16, 16, 128)
    mid = jnp.stack([mid, other], axis=1).reshape(512, 128).astype(BF)
    up = jnp.dot(up_left[0], mid, preferred_element_type=F32)
    down = jnp.dot(down_left[0], mid, preferred_element_type=F32)
    lane = lax.broadcasted_iota(jnp.int32, (512, 128), 1)
    both = jnp.where(lane < 32, up, down).reshape(32, 2, 8, 128)
    top = both[:, 0].reshape(256, 128)
    low = pltpu.roll(both[:, 1].reshape(256, 128), 64, 1)
    lane = lax.broadcasted_iota(jnp.int32, (256, 128), 1)
    packed = jnp.where(lane < 64, top, low).reshape(2, 8, 16, 128)
    packed = jnp.stack([packed[:, near] for near in range(8)])
    out_ref[...] = packed.reshape(16, 16, 128).astype(BF)


def unpack_kernel(got_ref, *refs):
    *moments, up_ref, down_ref = refs
    for own_ref, out_ref in zip(moments[:4], moments[4:]):
        out_ref[...] = own_ref[...]
    got = got_ref[...].astype(F32).reshape(8, 2, 16, 128)
    got = jnp.stack([got[:, far] for far in range(2)]).reshape(256, 128)
    low = pltpu.roll(got, 64, 1)
    rows = jnp.stack([got.reshape(32, 8, 128), low.reshape(32, 8, 128)], axis=1)
    rows = rows.reshape(512, 128)
    up_ref[...] = rows[:, :32].reshape(32, 16, 32).astype(BF)
    down_ref[...] = pltpu.roll(rows, 96, 1)[:, :32].reshape(32, 16, 32).astype(BF)


def per_device(
    up_partials,
    down_partials,
    up_left,
    up_right,
    down_left,
    down_right,
    up_first,
    up_second,
    down_first,
    down_second,
):
    core, part = lax.axis_index("core"), lax.axis_index("y")

    sent = jnp.where(core == 0, down_partials[0], up_partials[0])
    got = lax.ppermute(sent, "core", [(0, 1), (1, 0)])
    left = jnp.where(core == 0, up_left[0], down_left[0]).reshape(32, 2, 8, 512)
    left = lax.dynamic_index_in_dim(left, part, 1, keepdims=False).reshape(2, 8, 16, 512)
    left = left.transpose(1, 0, 2, 3).reshape(256, 512)
    got, left = lax.optimization_barrier((got, left))
    chunks = call(
        chunk_kernel,
        jax.ShapeDtypeStruct((16, 8, 16, 128), BF),
        up_partials,
        down_partials,
        got,
    )
    got = exchange(chunks, ("h", "x", "y"))
    summed = call(sum_kernel, jax.ShapeDtypeStruct((16, 16, 128), BF), got)
    grad = exchange(summed, ("near", "far")).reshape(256, 128)
    half = jnp.einsum("pr,pq->rq", left, grad, preferred_element_type=F32)
    half = exchange(half.astype(BF).reshape(16, 32, 128), DP)

    rows = jax.ShapeDtypeStruct((1, 32, 512), F32)
    *moments, mid = call(
        middle_kernel,
        [rows] * 4 + [jax.ShapeDtypeStruct((16, 16, 128), BF)],
        half,
        up_right,
        down_right,
        up_first,
        up_second,
        down_first,
        down_second,
    )
    mid = exchange(mid, DP)
    packed = call(
        back_kernel, jax.ShapeDtypeStruct((16, 16, 128), BF), mid, up_left, down_left
    )
    packed = exchange(packed.reshape(32, 8, 128), ("near", "far", "h")).reshape(16, 16, 128)
    update = jax.ShapeDtypeStruct((32, 16, 32), BF)
    return tuple(call(unpack_kernel, [rows] * 4 + [update] * 2, packed, *moments))


def solution(mesh):
    mesh = Mesh(mesh.devices.reshape(4, 2, 2, 2, 8, 2), ("x", "y", "core", "far", "near", "h"))
    blocks, rows = P(MP, None, None), P(MP, DP, None)
    partials, update = P(DP, None, MP, None), P(None, MP, DP)
    return jax.shard_map(
        per_device,
        mesh=mesh,
        in_specs=(partials, partials, blocks, blocks, blocks, blocks, rows, rows, rows, rows),
        out_specs=(rows, rows, rows, rows, update, update),
        check_vma=False,
    )
```

```python
import jax
import jax.numpy as jnp
from jax import lax
from jax.experimental import pallas as pl
from jax.experimental.pallas import tpu as pltpu
from jax.sharding import Mesh
from jax.sharding import PartitionSpec as P

CORR_FIRST = 1.0 - 0.9**50 * 0.9**50
CORR_SECOND = 1.0 - 0.95**50 * 0.95**50
BF = jnp.bfloat16
F32 = jnp.float32
DP = ("x", "y", "core")
MP = ("far", "near", "h")
PARAMS = pltpu.CompilerParams(vmem_limit_bytes=16 * 2**20)


def exchange(x, axis):
    return lax.all_to_all(x, axis, 0, 0, tiled=True)


def call(kernel, out_shape, *args):
    return pl.pallas_call(kernel, out_shape=out_shape, compiler_params=PARAMS)(*args)


def chunk_kernel(up_ref, down_ref, got_ref, out_ref):
    def chunks(own_ref):
        for at in range(4):
            lanes = pl.ds(128 * at, 128)
            total = own_ref[0, :, :, lanes].astype(F32) + got_ref[:, :, lanes].astype(F32)
            total = total.reshape(16, 2, 2, 8, 128)
            for half in range(2):
                for odd in range(2):
                    part = total[:, odd, half].reshape(8, 16, 128)
                    out_ref[8 * odd + 2 * at + 1 * half] = part.astype(BF)

    core = lax.axis_index("core")

    @pl.when(core == 0)
    def _():
        chunks(up_ref)

    @pl.when(core == 1)
    def _():
        chunks(down_ref)


def sum_kernel(got_ref, out_ref):
    sums = []
    for odd in range(2):
        total = 0.0
        for at in range(4):
            for half in range(2):
                total = total + got_ref[8 * odd + 2 * at + 1 * half].astype(F32)
        sums.append(total.reshape(16, 8, 128))
    out = jnp.stack(sums, axis=1).reshape(2, 8, 16, 128)
    out = jnp.stack([out[:, near] for near in range(8)])
    out_ref[...] = out.reshape(16, 16, 128).astype(BF)


def middle_kernel(
    half_ref,
    up_right,
    down_right,
    up_first,
    up_second,
    down_first,
    down_second,
    up_first_new,
    up_second_new,
    down_first_new,
    down_second_new,
    mid_ref,
):
    sides = (
        (up_right, up_first, up_second, up_first_new, up_second_new),
        (down_right, down_first, down_second, down_first_new, down_second_new),
    )
    rotated = []
    for k in range(2):
        tiles = [
            (half_ref[4 * at + k].astype(F32) + half_ref[4 * at + 2 + k].astype(F32)).astype(BF)
            for at in range(4)
        ]
        rows = jnp.concatenate(tiles, axis=1)
        rotated.append(jnp.dot(rows, sides[k][0][0], preferred_element_type=F32))
    directions = []
    for k in range(2):
        _, first, second, first_out, second_out = sides[k]
        first_new = 0.9 * first[0] + 0.1 * rotated[k]
        second_new = 0.95 * second[0] + 0.05 * rotated[k] * rotated[k]
        first_out[0] = first_new
        second_out[0] = second_new
        direction = first_new / CORR_FIRST / (jnp.sqrt(second_new / CORR_SECOND) + 1e-08)
        directions.append(direction.astype(BF))
    mids = [
        lax.dot_general(
            directions[k],
            sides[k][0][0],
            (((1,), (1,)), ((), ())),
            preferred_element_type=F32,
        )
        for k in range(2)
    ]
    lane = lax.broadcasted_iota(jnp.int32, (16, 128), 1)
    for at in range(4):
        pieces = [
            mids[k][16 * rh : 16 * rh + 16, 128 * at : 128 * at + 128]
            for rh in range(2)
            for k in range(2)
        ]
        for w in range(4):
            rolled = [
                piece if g == w else pltpu.roll(piece, (32 * (g - w)) % 128, 1)
                for g, piece in enumerate(pieces)
            ]
            packed = jnp.where(
                lane < 64,
                jnp.where(lane < 32, rolled[0], rolled[1]),
                jnp.where(lane < 96, rolled[2], rolled[3]),
            )
            mid_ref[8 * (w % 2) + 2 * at + w // 2] = packed.astype(BF)


def back_kernel(mid_ref, up_left, down_left, out_ref):
    mid = jnp.stack([mid_ref[8 * (at % 2) + at // 2] for at in range(16)]).astype(F32)
    other = pltpu.roll(mid.reshape(256, 128), 64, 1).reshape(16, 16, 128)
    mid = jnp.stack([mid, other], axis=1).reshape(512, 128).astype(BF)
    up = jnp.dot(up_left[0], mid, preferred_element_type=F32)
    down = jnp.dot(down_left[0], mid, preferred_element_type=F32)
    lane = lax.broadcasted_iota(jnp.int32, (512, 128), 1)
    both = jnp.where(lane < 32, up, down).reshape(32, 2, 8, 128)
    top = both[:, 0].reshape(256, 128)
    low = pltpu.roll(both[:, 1].reshape(256, 128), 64, 1)
    lane = lax.broadcasted_iota(jnp.int32, (256, 128), 1)
    packed = jnp.where(lane < 64, top, low).reshape(2, 8, 16, 128)
    packed = jnp.stack([packed[:, near] for near in range(8)])
    out_ref[...] = packed.reshape(16, 16, 128).astype(BF)


def unpack_kernel(got_ref, *refs):
    *moments, up_ref, down_ref = refs
    for own_ref, out_ref in zip(moments[:4], moments[4:]):
        out_ref[...] = own_ref[...]
    got = got_ref[...].astype(F32).reshape(8, 2, 16, 128)
    got = jnp.stack([got[:, far] for far in range(2)]).reshape(256, 128)
    low = pltpu.roll(got, 64, 1)
    rows = jnp.stack([got.reshape(32, 8, 128), low.reshape(32, 8, 128)], axis=1)
    rows = rows.reshape(512, 128)
    up_ref[...] = rows[:, :32].reshape(32, 16, 32).astype(BF)
    down_ref[...] = pltpu.roll(rows, 96, 1)[:, :32].reshape(32, 16, 32).astype(BF)


def per_device(
    up_partials,
    down_partials,
    up_left,
    up_right,
    down_left,
    down_right,
    up_first,
    up_second,
    down_first,
    down_second,
):
    core, part = lax.axis_index("core"), lax.axis_index("y")

    sent = jnp.where(core == 0, down_partials[0], up_partials[0])
    got = lax.ppermute(sent, "core", [(0, 1), (1, 0)])
    left = jnp.where(core == 0, up_left[0], down_left[0]).reshape(32, 2, 8, 512)
    left = lax.dynamic_index_in_dim(left, part, 1, keepdims=False).reshape(2, 8, 16, 512)
    left = left.transpose(1, 0, 2, 3).reshape(256, 512)
    got, left = lax.optimization_barrier((got, left))
    chunks = call(
        chunk_kernel,
        jax.ShapeDtypeStruct((16, 8, 16, 128), BF),
        up_partials,
        down_partials,
        got,
    )
    got = exchange(chunks, ("h", "x", "y"))
    summed = call(sum_kernel, jax.ShapeDtypeStruct((16, 16, 128), BF), got)
    grad = exchange(summed, ("near", "far")).reshape(256, 128)
    half = jnp.einsum("pr,pq->rq", left, grad, preferred_element_type=F32)
    half = exchange(half.astype(BF).reshape(16, 32, 128), DP)

    rows = jax.ShapeDtypeStruct((1, 32, 512), F32)
    *moments, mid = call(
        middle_kernel,
        [rows] * 4 + [jax.ShapeDtypeStruct((16, 16, 128), BF)],
        half,
        up_right,
        down_right,
        up_first,
        up_second,
        down_first,
        down_second,
    )
    mid = exchange(mid, ("core", "x", "y"))
    packed = call(
        back_kernel, jax.ShapeDtypeStruct((16, 16, 128), BF), mid, up_left, down_left
    )
    packed = exchange(packed.reshape(32, 8, 128), ("near", "far", "h")).reshape(16, 16, 128)
    update = jax.ShapeDtypeStruct((32, 16, 32), BF)
    return tuple(call(unpack_kernel, [rows] * 4 + [update] * 2, packed, *moments))


def solution(mesh):
    mesh = Mesh(mesh.devices.reshape(4, 2, 2, 2, 8, 2), ("x", "y", "core", "far", "near", "h"))
    blocks, rows = P(MP, None, None), P(MP, DP, None)
    partials, update = P(DP, None, MP, None), P(None, MP, DP)
    return jax.shard_map(
        per_device,
        mesh=mesh,
        in_specs=(partials, partials, blocks, blocks, blocks, blocks, rows, rows, rows, rows),
        out_specs=(rows, rows, rows, rows, update, update),
        check_vma=False,
    )
```
